32 devices in a mesh: seq: 4 (over z), exp: 8 (over y, x, core).
Axes of the slice: x: 2, y: 2, z: 4, core: 2. Of those that a mesh axis runs over, the one named last changes fastest.
Arguments:
- streams: bfloat16 [2048, 4, 3584], P(('seq', 'exp')), may hold values from -6 to 6
- phi_matrix: bfloat16 [24, 14336], replicated, may hold values from -0.046875 to 0.046875
- mix_scale: float32 [3], replicated, may hold values from 0.5 to 2
- mix_bias: float32 [24], replicated, may hold values from -1 to 1
- router: bfloat16 [32, 3584], replicated, may hold values from -0.09375 to 0.09375
- expert_index_table: int32 [2048, 8], P(('seq', 'exp')), may hold values from 0 to 31, all different within a row; in each aligned block of 64 rows (0 to 63, 64 to 127, ...) at most 20 rows name the same one
- w_gate: bfloat16 [32, 3584, 2048], P('exp', None, 'seq'), may hold values from -0.09375 to 0.09375
- w_up: bfloat16 [32, 3584, 2048], P('exp', None, 'seq'), may hold values from -0.09375 to 0.09375
- down_weight: bfloat16 [32, 2048, 3584], P('exp', 'seq'), may hold values from -0.125 to 0.125
Outputs:
- new_streams: bfloat16 [2048, 4, 3584], P(('seq', 'exp'))
The draws below stay inside these ranges and needn't reach their ends.
Inputs may be any that keep to these rules, and one draw needn't show every extreme that they name: `expert_index_table`: each row names 8 different experts; among the 64 rows of one device (aligned blocks of 64 rows) no expert is named by more than 20 rows, a bound that some block reaches; every expert is named somewhere.
All inputs are finite; a program needn't handle non-finite values.
Results may differ from the reference program's by a relative error of at most 0.012.
Values may be sent and summed in bfloat16 or wider, within the bound.
A program may use at most 192 MiB of HBM per device.

```python
import math
import jax
import jax.numpy as jnp
import numpy as np
from jax import lax

D = 3584
FF = 2048
STREAMS = 4
TOPK = 8
BALANCE_SWEEPS = 20
EXPERTS = 32
TOK_DEV = 64
TOKENS = 2048
CAP = 20
MIXES = 24
N_SEQ = 4
N_EXP = 8


def shard_levels(rng, dims, pieces, low, top_value):
    gain, own = 1.0, jax.random.fold_in(rng, 6)
    for axis_at, shards_of in pieces:
        draws = jnp.exp(jax.random.uniform(jax.random.fold_in(own, axis_at), (shards_of,), jnp.float32, low / len(pieces), top_value / len(pieces)))
        gain = gain * jnp.repeat(draws, dims[axis_at] // shards_of).reshape([-1 if axis == axis_at else 1 for axis in range(len(dims))])
    return gain


def deal_out(rng, own, number, rows, amount, top, most, slope):
    sequence = jax.random.permutation(rng, amount)
    crowded, ordinary = load_shares(amount, rows * top, most, slope, True), load_shares(amount, rows * top, most, slope, False)
    places = jnp.arange(amount)

    def named(lengths, offset_by):
        used = int((lengths > 0).sum())
        fixed = max(1, used // 4)
        shifted = fixed + (places - fixed + offset_by * (used - fixed)) % max(1, amount - fixed)
        return jnp.zeros((amount,), jnp.int32).at[sequence[jnp.where(places < fixed, places, shifted)]].set(jnp.asarray(lengths, jnp.int32))

    lengths = jnp.where(number % 4 == 0, named(crowded, number // 4), named(ordinary, number - number // 4 - 1))
    mixed = jax.random.permutation(jax.random.fold_in(own, 3), amount)
    donor, taker = mixed[0:amount // 2 * 2:2], mixed[1:amount // 2 * 2:2]
    margin = jnp.minimum(lengths[donor] - 1, most - lengths[taker]) // 2
    margin = jnp.where((donor == sequence[0]) | (taker == sequence[0]) | (lengths[taker] == 0), 0, jnp.maximum(margin, 0))
    shifted = jax.random.randint(jax.random.fold_in(own, 4), (amount // 2,), 0, 1 << 20) % (margin + 1)
    lengths = lengths.at[donor].add(-shifted).at[taker].add(shifted)
    members = jnp.searchsorted(jnp.cumsum(lengths), jnp.arange(rows * top), side="right").astype(jnp.int32)
    listing = members.reshape(top, rows).T
    listing = listing[jax.random.permutation(jax.random.fold_in(own, 1), rows)]
    offset_by = jax.random.randint(jax.random.fold_in(own, 2), (rows, 1), 0, top)
    return jnp.take_along_axis(listing, (jnp.arange(top)[None, :] + offset_by) % top, axis=1)


def load_shares(number_of, total, most, skew, full):
    portions = [(1 << 20) // math.isqrt(grade ** skew) + 1 for grade in range(1, number_of + 1)]
    largest = most if full else min(most, max(-(-total // number_of), total * portions[0] // sum(portions)))
    least = 1 if total - largest >= number_of - 1 else 0
    holding, surplus = [largest] + [least] * (number_of - 1), total - largest - least * (number_of - 1)
    while surplus > 0:
        movable = [i for i in range(1, number_of) if holding[i] < largest] or [i for i in range(1, number_of) if holding[i] < most]
        pool, remaining = sum([portions[i] for i in movable]), surplus
        for i in movable:
            extra = min(most - holding[i], max(1, remaining * portions[i] // pool), surplus)
            holding[i] = holding[i] + extra
            surplus = surplus - extra
    return np.array(holding)


def bell_draw(rng, dims, scale, reach, cuts=(), kind=jnp.bfloat16):
    array = scale * jax.random.normal(rng, dims, jnp.float32)
    if cuts:
        array = array * shard_levels(rng, dims, cuts, -0.22, 0.18)
    return jnp.clip(array, -reach, reach).astype(kind)


def setup_inputs(seed: int = 0) -> dict:
    arg_keys = jax.random.split(jax.random.key(seed), 10)
    streams = bell_draw(arg_keys[0], (TOKENS, STREAMS, D), 1.0, 6.0, ((0, 32),))
    phi_matrix = bell_draw(arg_keys[1], (MIXES, STREAMS * D), (STREAMS * D) ** -0.5, 0.046875)
    mix_scale = jnp.clip(jnp.exp(jax.random.uniform(arg_keys[2], (3,), jnp.float32, math.log(0.5), math.log(2.0))), 0.5, 2.0)
    mix_bias = jnp.clip(jax.random.uniform(arg_keys[3], (MIXES,), jnp.float32, -1.0, 1.0), -1.0, 1.0)
    router = bell_draw(arg_keys[4], (EXPERTS, D), D ** -0.5, 0.09375)
    expert_index_table_keys = jax.random.split(jax.random.fold_in(arg_keys[5], 1), TOKENS // TOK_DEV)
    expert_index_table_turns = jax.random.permutation(jax.random.fold_in(arg_keys[5], 3), TOKENS // TOK_DEV)
    expert_index_table = jax.vmap(lambda own, number: deal_out(jax.random.fold_in(arg_keys[5], 2), own, number, TOK_DEV, EXPERTS, TOPK, CAP, 2))(expert_index_table_keys, expert_index_table_turns).reshape((TOKENS, TOPK))
    w_gate = bell_draw(arg_keys[6], (EXPERTS, D, FF), D ** -0.5, 0.09375, ((0, 8), (2, 4)))
    w_up = bell_draw(arg_keys[7], (EXPERTS, D, FF), D ** -0.5, 0.09375, ((0, 8), (2, 4)))
    down_weight = bell_draw(arg_keys[8], (EXPERTS, FF, D), FF ** -0.5, 0.125, ((0, 8), (1, 4)))
    return dict(streams=streams, phi_matrix=phi_matrix, mix_scale=mix_scale, mix_bias=mix_bias, router=router, expert_index_table=expert_index_table, w_gate=w_gate, w_up=w_up, down_weight=down_weight)


def mix_coefficients(streams, phi_matrix, mix_scale, mix_bias):
    count = streams.shape[1]
    flat = streams.astype(jnp.float32).reshape(streams.shape[0], -1)
    normed = flat * lax.rsqrt(lax.optimization_barrier(jnp.mean(flat * flat, axis=1, keepdims=True)) + 1e-06)
    normed = normed.astype(jnp.bfloat16)
    coeffs = lax.dot_general(normed, phi_matrix, (((1,), (1,)), ((), ())), preferred_element_type=jnp.float32)
    pre = jax.nn.sigmoid(mix_scale[0] * coeffs[:, :count] + mix_bias[:count])
    post = 2.0 * jax.nn.sigmoid(mix_scale[1] * coeffs[:, count:2 * count] + mix_bias[count:2 * count])
    logits = mix_scale[2] * coeffs[:, 2 * count:] + mix_bias[2 * count:]
    mixing = jnp.exp(logits).reshape(-1, count, count)
    for sweep_step in range(BALANCE_SWEEPS):
        mixing = mixing / lax.optimization_barrier(jnp.sum(mixing, axis=2, keepdims=True))
        mixing = mixing / lax.optimization_barrier(jnp.sum(mixing, axis=1, keepdims=True))
    return (pre, post, mixing)

def mix_input(streams, pre):
    total = pre[:, 0, None] * streams[:, 0, :].astype(jnp.float32)
    for stream in range(1, streams.shape[1]):
        total = total + pre[:, stream, None] * streams[:, stream, :].astype(jnp.float32)
    return total.astype(jnp.bfloat16)

def mix_output(streams, mixing, post, moe_out):
    rows = []
    for target in range(streams.shape[1]):
        total = mixing[:, target, 0, None] * streams[:, 0, :].astype(jnp.float32)
        for source in range(1, streams.shape[1]):
            total = total + mixing[:, target, source, None] * streams[:, source, :].astype(jnp.float32)
        rows.append(total + post[:, target, None] * moe_out)
    return jnp.stack(rows, axis=1).astype(jnp.bfloat16)

def route_gates(layer_in, router, expert_index_table):
    logits = lax.dot_general(layer_in, router, (((1,), (1,)), ((), ())), preferred_element_type=jnp.float32)
    affinity = jax.nn.sigmoid(logits)
    chosen = jnp.take_along_axis(affinity, expert_index_table, axis=1)
    return 2.5 * chosen / lax.optimization_barrier(jnp.sum(chosen, axis=1, keepdims=True))

def reference(streams, phi_matrix, mix_scale, mix_bias, router, expert_index_table, w_gate, w_up, down_weight):
    pre, post, mixing = mix_coefficients(streams, phi_matrix, mix_scale, mix_bias)
    layer_in = mix_input(streams, pre)
    gates = route_gates(layer_in, router, expert_index_table)
    limit = N_SEQ * N_EXP * CAP
    group_width = FF // N_SEQ
    width = streams.shape[2]

    def one_expert(total, inputs):
        weight_gate, weight_up, weight_down, expert = inputs
        hits = expert_index_table == expert
        chosen = jnp.any(hits, axis=1)
        weight = lax.optimization_barrier(jnp.sum(jnp.where(hits, gates, 0.0), axis=1))
        index = jnp.nonzero(chosen, size=limit, fill_value=0)[0].astype(jnp.int32)
        valid = (jnp.arange(limit) < jnp.sum(chosen.astype(jnp.int32))).astype(jnp.float32)
        rows = layer_in[index]
        gate_part = jnp.dot(rows, weight_gate, preferred_element_type=jnp.float32)
        up_part = jnp.dot(rows, weight_up, preferred_element_type=jnp.float32)
        hidden = (jax.nn.silu(gate_part) * up_part).astype(jnp.bfloat16)
        output = jnp.zeros((limit, width), jnp.float32)
        for group in range(N_SEQ):
            part = jnp.dot(hidden[:, group * group_width:(group + 1) * group_width], weight_down[group * group_width:(group + 1) * group_width], preferred_element_type=jnp.float32).astype(jnp.bfloat16)
            part = lax.optimization_barrier(part)
            output = output + part.astype(jnp.float32)
        total = total.at[index].add((weight[index] * valid)[:, None] * output)
        return (total, None)
    experts = jnp.arange(EXPERTS, dtype=jnp.int32)
    moe_out, ignored_entry = lax.scan(one_expert, jnp.zeros((streams.shape[0], width), jnp.float32), (w_gate, w_up, down_weight, experts))
    return mix_output(streams, mixing, post, moe_out)
```

```python
import functools

import jax
import jax.numpy as jnp
from jax import lax
from jax.experimental import pallas as pl
from jax.experimental.pallas import tpu as pltpu
from jax.sharding import PartitionSpec as P

BALANCE_SWEEPS = 20
EXPERTS = 32
CAP = 20
MESH = pl.DeviceIdType.MESH


def mix_coefficients(streams, phi_matrix, mix_scale, mix_bias):
    count = streams.shape[1]
    flat = streams.astype(jnp.float32).reshape(streams.shape[0], -1)
    normed = flat * lax.rsqrt(jnp.mean(flat * flat, axis=1, keepdims=True) + 1e-06)
    normed = normed.astype(jnp.bfloat16)
    coeffs = lax.dot_general(
        normed, phi_matrix, (((1,), (1,)), ((), ())), preferred_element_type=jnp.float32
    )
    pre = jax.nn.sigmoid(mix_scale[0] * coeffs[:, :count] + mix_bias[:count])
    post = 2.0 * jax.nn.sigmoid(
        mix_scale[1] * coeffs[:, count : 2 * count] + mix_bias[count : 2 * count]
    )
    logits = mix_scale[2] * coeffs[:, 2 * count :] + mix_bias[2 * count :]
    mixing = jnp.exp(logits).reshape(-1, count, count)
    for sweep_step in range(BALANCE_SWEEPS):
        mixing = mixing / jnp.sum(mixing, axis=2, keepdims=True)
        mixing = mixing / jnp.sum(mixing, axis=1, keepdims=True)
    return (pre, post, mixing)


def mix_input(streams, pre):
    total = pre[:, 0, None] * streams[:, 0, :].astype(jnp.float32)
    for stream in range(1, streams.shape[1]):
        total = total + pre[:, stream, None] * streams[:, stream, :].astype(jnp.float32)
    return total.astype(jnp.bfloat16)


def mix_output(streams, mixing, post, moe_out):
    rows = []
    for target in range(streams.shape[1]):
        total = mixing[:, target, 0, None] * streams[:, 0, :].astype(jnp.float32)
        for source in range(1, streams.shape[1]):
            total = total + mixing[:, target, source, None] * streams[:, source, :].astype(
                jnp.float32
            )
        rows.append(total + post[:, target, None] * moe_out)
    return jnp.stack(rows, axis=1).astype(jnp.bfloat16)


def route_gates(layer_in, router, expert_index_table):
    logits = lax.dot_general(
        layer_in, router, (((1,), (1,)), ((), ())), preferred_element_type=jnp.float32
    )
    affinity = jax.nn.sigmoid(logits)
    chosen = jnp.take_along_axis(affinity, expert_index_table, axis=1)
    return 2.5 * chosen / jnp.sum(chosen, axis=1, keepdims=True)


def slot_ranks(expert_index_table):
    flat = expert_index_table.reshape(-1)
    onehot = (flat[:, None] == lax.iota(jnp.int32, EXPERTS)[None, :]).astype(jnp.int32)
    prior_value = jnp.cumsum(onehot, axis=0) - onehot
    return jnp.sum(prior_value * onehot, axis=1).reshape(expert_index_table.shape)


def expert_block(blocks, w_gate, w_up, down_weight):
    count, local, slots, width = blocks.shape
    rows = blocks.transpose(1, 0, 2, 3).reshape(local, count * slots, width)
    gate_part = jnp.einsum("erd,edf->erf", rows, w_gate, preferred_element_type=jnp.float32)
    up_part = jnp.einsum("erd,edf->erf", rows, w_up, preferred_element_type=jnp.float32)
    hidden = (jax.nn.silu(gate_part) * up_part).astype(jnp.bfloat16)
    part = jnp.einsum(
        "erf,efd->erd", hidden, down_weight, preferred_element_type=jnp.float32
    ).astype(jnp.bfloat16)
    return part.reshape(local, count, slots, width).transpose(1, 0, 2, 3)


def weigh_slots(returned_rows, targets, gates):
    selected_slot = jnp.take(returned_rows, targets.reshape(-1), axis=0).astype(jnp.float32)
    selected_slot = selected_slot.reshape(
        targets.shape[0], targets.shape[1], returned_rows.shape[1]
    )
    return jnp.sum(gates[:, :, None] * selected_slot, axis=1)


def body(
    streams, phi_matrix, mix_scale, mix_bias, router, expert_index_table, w_gate, w_up, down_weight
):
    pre, post, mixing = mix_coefficients(streams, phi_matrix, mix_scale, mix_bias)
    layer_in = mix_input(streams, pre)
    width = layer_in.shape[1]
    owners = lax.axis_size("exp")
    local = w_gate.shape[0]
    column_in, column_ids = (
        lax.all_gather(layer_in, "seq", axis=0, tiled=True),
        lax.all_gather(expert_index_table, "seq", axis=0, tiled=True),
    )
    sources = lax.axis_size("seq")
    tok_count = layer_in.shape[0]
    topk = expert_index_table.shape[1]
    gates = route_gates(column_in, router, column_ids)
    ranks = jax.vmap(slot_ranks)(column_ids.reshape(sources, tok_count, topk)).reshape(
        column_ids.shape
    )
    source_lookup = (lax.iota(jnp.int32, sources * tok_count) // tok_count)[:, None]
    targets = (column_ids * sources + source_lookup) * CAP + ranks
    places = lax.iota(jnp.int32, EXPERTS * sources * CAP)
    dispatch = jnp.any(places[:, None, None] == targets[None, :, :], axis=2).astype(jnp.bfloat16)
    send = jnp.dot(dispatch, column_in, preferred_element_type=jnp.float32).astype(jnp.bfloat16)
    send = send.reshape(owners, local, sources * CAP, width)
    part = expert_block(
        lax.all_to_all(send, "exp", split_axis=0, concat_axis=0, tiled=True),
        w_gate,
        w_up,
        down_weight,
    )
    returned = lax.all_to_all(part, "exp", split_axis=0, concat_axis=0, tiled=True)
    weighted = weigh_slots(returned.reshape(-1, width), targets, gates)
    moe_out = lax.psum_scatter(
        weighted.astype(jnp.bfloat16), "seq", scatter_dimension=0, tiled=True
    ).astype(jnp.float32)
    return mix_output(streams, mixing, post, moe_out)


def swap(exp, bit):
    side = lax.rem(exp // bit, 2)
    return exp + bit - 2 * bit * side


def greet(peers):
    barrier = pltpu.get_barrier_semaphore()
    for peer in peers:
        pl.semaphore_signal(barrier, inc=1, device_id=peer, device_id_type=MESH)
    pl.semaphore_wait(barrier, len(peers))


def place(planes, exps):
    z, e = lax.axis_index("seq"), lax.axis_index("exp")
    core, x, y = swap(e, 1), swap(e, 2), swap(e, 4)
    both = swap(x, 4)
    return z, e, core, x, y, both


def gather_kernel(planes, exps, block, out, s_z, r_z, s_1, r_1, s_2, r_2, s_c, r_c, s_own):
    z, e, core, x, y, both = place(planes, exps)
    half_rows = block.shape[0] // 2
    first, second = (x, y), (y, x)
    greet([(lax.rem(z + d, planes), e) for d in range(1, planes)] + [(z, x), (z, y), (z, core)])
    started = []

    def rows(half):
        return pl.ds(half * half_rows, half_rows)

    def push(src, plane, exp, half, send, recv, target):
        copy = pltpu.make_async_remote_copy(
            src_ref=src,
            dst_ref=out.at[plane * exps + exp, rows(half)],
            send_sem=send,
            recv_sem=recv,
            device_id=target,
            device_id_type=MESH,
        )
        copy.start()
        started.append(copy)

    def arrive(plane, exp, half, sem):
        spot = out.at[plane * exps + exp, rows(half)]
        pltpu.make_async_copy(spot, spot, sem).wait()

    def plane_at(k):
        return lax.rem(z + planes - k, planes)

    def local(k, exp, half):
        if k == 0 and exp is e:
            return block.at[rows(half)]
        return out.at[plane_at(k) * exps + exp, rows(half)]

    def across(k, exp, half, index):
        push(local(k, exp, half), plane_at(k), exp, half, s_c.at[k, half, index], r_c.at[k, half, index], (z, core))

    def spread_own(k):
        for half in (0, 1):
            if k:
                arrive(plane_at(k), e, half, r_z.at[k - 1, half])
            push(local(k, e, half), plane_at(k), e, half, s_1.at[k, half], r_1.at[k, half], (z, first[half]))
            push(local(k, e, half), plane_at(k), e, half, s_2.at[k, half, 0], r_2.at[k, half, 0], (z, second[half]))
            across(k, e, half, 0)

    def spread_first(k):
        for half in (0, 1):
            arrive(plane_at(k), first[half], half, r_1.at[k, half])
            push(local(k, first[half], half), plane_at(k), first[half], half, s_2.at[k, half, 1], r_2.at[k, half, 1], (z, second[half]))
            across(k, first[half], half, 1)

    def spread_second(k):
        for half in (0, 1):
            for index, exp in enumerate((second[half], both)):
                arrive(plane_at(k), exp, half, r_2.at[k, half, index])
                across(k, exp, half, 2 + index)

    own = pltpu.make_async_copy(block, out.at[z * exps + e], s_own)
    own.start()
    for d in range(1, planes):
        for half in (0, 1):
            push(block.at[rows(half)], z, e, half, s_z.at[d - 1, half], r_z.at[d - 1, half], (lax.rem(z + d, planes), e))
    spread_own(0)
    for k in range(1, planes + 2):
        if k < planes:
            spread_own(k)
        if k - 1 < planes:
            spread_first(k - 1)
        if k >= 2:
            spread_second(k - 2)
    for k in range(planes):
        for half in (0, 1):
            here = (core, swap(first[half], 1), swap(second[half], 1), swap(both, 1))
            for index, exp in enumerate(here):
                arrive(plane_at(k), exp, half, r_c.at[k, half, index])
    for copy in started:
        copy.wait_send()
    own.wait()


def gather_tokens(block, planes, exps):
    dma = pltpu.SemaphoreType.DMA
    shapes = [(planes - 1, 2), (planes, 2), (planes, 2, 2), (planes, 2, 4)]
    return pl.pallas_call(
        functools.partial(gather_kernel, planes, exps),
        out_shape=jax.ShapeDtypeStruct((planes * exps,) + block.shape, block.dtype),
        in_specs=[pl.BlockSpec(memory_space=pl.ANY)],
        out_specs=pl.BlockSpec(memory_space=pl.ANY),
        scratch_shapes=[dma(shape) for shape in shapes for way in range(2)] + [dma],
        compiler_params=pltpu.CompilerParams(collective_id=0, has_side_effects=True),
        name="gather_tokens",
    )(block)


def scatter_kernel(planes, exps, parts, out, held, in_c, in_2, in_1, in_z,
                   s_own, s_c, r_c, s_2, r_2, s_1, r_1, s_z, r_z):
    z, e, core, x, y, both = place(planes, exps)
    tokens, width = out.shape
    half_rows = tokens // 2
    step = 512 if width % 512 == 0 else width
    first, second = (x, y), (y, x)
    greet([(lax.rem(z + d, planes), e) for d in range(1, planes)] + [(z, x), (z, y), (z, core)])
    started = []

    def rows(half):
        return pl.ds(half * half_rows, half_rows)

    def push(src, dst, send, recv, target):
        copy = pltpu.make_async_remote_copy(
            src_ref=src, dst_ref=dst, send_sem=send, recv_sem=recv, device_id=target, device_id_type=MESH
        )
        copy.start()
        started.append(copy)

    def arrive(spot, sem):
        pltpu.make_async_copy(spot, spot, sem).wait()

    def add(total, term):
        def one(i, carry):
            columns = pl.ds(pl.multiple_of(i * step, step), step)
            total[:, columns] = (
                total[:, columns].astype(jnp.float32) + term[:, columns].astype(jnp.float32)
            ).astype(total.dtype)
            return carry

        lax.fori_loop(0, width // step, one, 0)

    def plane_at(k):
        return lax.rem(z + k, planes)

    def dests(half):
        return (both, second[half], first[half], e)

    order = [k for k in range(1, planes)] + [0]
    loads = {}
    for k in order:
        for half in (0, 1):
            for index, exp in enumerate(dests(half)):
                away = parts.at[plane_at(k) * exps + swap(exp, 1), rows(half)]
                push(away, in_c.at[k, half, index], s_c.at[k, half, index], r_c.at[k, half, index], (z, core))
                load = pltpu.make_async_copy(
                    parts.at[plane_at(k) * exps + exp, rows(half)], held.at[k, half, index], s_own.at[k, half, index]
                )
                load.start()
                loads[k, half, index] = load

    def merge_core(k):
        for half in (0, 1):
            for index in range(4):
                loads[k, half, index].wait()
                arrive(in_c.at[k, half, index], r_c.at[k, half, index])
                add(held.at[k, half, index], in_c.at[k, half, index])
                if index < 2:
                    push(held.at[k, half, index], in_2.at[k, half, index], s_2.at[k, half, index], r_2.at[k, half, index], (z, second[half]))

    def merge_second(k):
        for half in (0, 1):
            for index in (0, 1):
                arrive(in_2.at[k, half, index], r_2.at[k, half, index])
                add(held.at[k, half, 2 + index], in_2.at[k, half, index])
                if index == 0:
                    push(held.at[k, half, 2], in_1.at[k, half], s_1.at[k, half], r_1.at[k, half], (z, first[half]))

    def merge_first(k):
        for half in (0, 1):
            arrive(in_1.at[k, half], r_1.at[k, half])
            add(held.at[k, half, 3], in_1.at[k, half])
            if k:
                push(held.at[k, half, 3], in_z.at[k - 1, half], s_z.at[k - 1, half], r_z.at[k - 1, half], (plane_at(k), e))

    for turn in range(planes + 2):
        if turn < planes:
            merge_core(order[turn])
        if 1 <= turn <= planes:
            merge_second(order[turn - 1])
        if turn >= 2:
            merge_first(order[turn - 2])
    for k in range(1, planes):
        for half in (0, 1):
            arrive(in_z.at[k - 1, half], r_z.at[k - 1, half])
    for half in (0, 1):
        def one(i, carry):
            columns = pl.ds(pl.multiple_of(i * step, step), step)
            total = held[0, half, 3, :, columns].astype(jnp.float32)
            for k in range(1, planes):
                total = total + in_z[k - 1, half, :, columns].astype(jnp.float32)
            out[half * half_rows : (half + 1) * half_rows, columns] = total
            return carry

        lax.fori_loop(0, width // step, one, 0)
    for copy in started:
        copy.wait_send()


def scatter_sum(parts, planes, exps):
    blocks, tokens, width = parts.shape
    dma = pltpu.SemaphoreType.DMA
    half = (tokens // 2, width)
    shapes = [(planes, 2, 4), (planes, 2, 2), (planes, 2), (planes - 1, 2)]
    return pl.pallas_call(
        functools.partial(scatter_kernel, planes, exps),
        out_shape=jax.ShapeDtypeStruct((tokens, width), jnp.float32),
        in_specs=[pl.BlockSpec(memory_space=pl.ANY)],
        out_specs=pl.BlockSpec(memory_space=pltpu.VMEM),
        scratch_shapes=[pltpu.VMEM(shape + half, parts.dtype) for shape in [shapes[0]] + shapes]
        + [dma(shapes[0])]
        + [dma(shape) for shape in shapes for way in range(2)],
        compiler_params=pltpu.CompilerParams(
            collective_id=1, has_side_effects=True, vmem_limit_bytes=48 * 1024 * 1024
        ),
        name="scatter_sum",
    )(parts)


def expert_kernel(tokens, spread, collect, slot_gates, w_gate, w_up, w_down, out,
                  held, slots, hidden, in_sems, out_sems):
    groups, group_rows, width = held.shape
    own = pl.program_id(0)
    last = pl.num_programs(0) - 1
    room = slots.shape[1] // pl.num_programs(0)
    ff = hidden.shape[1]
    wide = 896 if width % 896 == 0 else width
    tall = 256 if ff % 256 == 0 else ff

    def load(g):
        return pltpu.make_async_copy(tokens.at[g, :, pl.ds(0, width)], held.at[g], in_sems.at[g])

    def store(g):
        return pltpu.make_async_copy(held.at[g], out.at[g], out_sems.at[g])

    @pl.when(own == 0)
    def dispatch():
        for g in range(groups):
            load(g).start()
        for g in range(groups):
            load(g).wait()

            def one(i, carry):
                columns = pl.ds(pl.multiple_of(i * wide, wide), wide)
                slots[g, :, columns] = jnp.dot(
                    spread[g], held[g, :, columns], preferred_element_type=jnp.float32
                ).astype(slots.dtype)
                return carry

            lax.fori_loop(0, width // wide, one, 0)

    mine = pl.ds(pl.multiple_of(own * room, room), room)
    for i in range(ff // tall):
        columns = pl.ds(i * tall, tall)
        rows = slots[:, mine, :].reshape(groups * room, width)
        gate_part = jnp.dot(rows, w_gate[0, :, columns], preferred_element_type=jnp.float32)
        up_part = jnp.dot(rows, w_up[0, :, columns], preferred_element_type=jnp.float32)
        hidden[:, columns] = (
            gate_part / (1.0 + jnp.exp(-gate_part)) * up_part * slot_gates[0]
        ).astype(hidden.dtype)

    def down(i, carry):
        columns = pl.ds(pl.multiple_of(i * wide, wide), wide)
        part = jnp.dot(hidden[...], w_down[0, :, columns], preferred_element_type=jnp.float32)
        slots[:, mine, columns] = part.astype(slots.dtype).reshape(groups, room, wide)
        return carry

    lax.fori_loop(0, width // wide, down, 0)

    @pl.when(own == last)
    def combine():
        for g in range(groups):

            def one(i, carry):
                columns = pl.ds(pl.multiple_of(i * wide, wide), wide)
                held[g, :, columns] = jnp.dot(
                    collect[g], slots[g, :, columns], preferred_element_type=jnp.float32
                ).astype(held.dtype)
                return carry

            lax.fori_loop(0, width // wide, one, 0)
            store(g).start()
        for g in range(groups):
            store(g).wait()


def run_experts(tokens, spread, slot_gates, w_gate, w_up, down_weight):
    groups, rows, _ = tokens.shape
    local, width, ff = w_gate.shape
    room = spread.shape[1] // local
    collect = spread.transpose(0, 2, 1)

    def whole(array):
        return pl.BlockSpec(array.shape, lambda i: (0,) * array.ndim, pipeline_mode=pl.Buffered(1))

    def each(array):
        return pl.BlockSpec((1,) + array.shape[1:], lambda i: (i, 0, 0))

    return pl.pallas_call(
        expert_kernel,
        grid=(local,),
        out_shape=jax.ShapeDtypeStruct((groups, rows, width), jnp.bfloat16),
        in_specs=[pl.BlockSpec(memory_space=pl.ANY), whole(spread), whole(collect)]
        + [each(a) for a in (slot_gates, w_gate, w_up, down_weight)],
        out_specs=pl.BlockSpec(memory_space=pl.ANY),
        scratch_shapes=[
            pltpu.VMEM((groups, rows, width), jnp.bfloat16),
            pltpu.VMEM((groups, local * room, width), jnp.bfloat16),
            pltpu.VMEM((groups * room, ff), jnp.bfloat16),
            pltpu.SemaphoreType.DMA((groups,)),
            pltpu.SemaphoreType.DMA((groups,)),
        ],
        compiler_params=pltpu.CompilerParams(
            dimension_semantics=("arbitrary",), vmem_limit_bytes=64 * 1024 * 1024 - 128 * 1024
        ),
        name="run_experts",
    )(tokens, spread, collect, slot_gates, w_gate, w_up, down_weight)


def dense_gates(layer_in, router, expert_index_table):
    logits = lax.dot_general(
        layer_in, router, (((1,), (1,)), ((), ())), preferred_element_type=jnp.float32
    )
    names = lax.iota(jnp.int32, EXPERTS)
    hits = jnp.any(expert_index_table[:, :, None] == names[None, None, :], axis=1)
    chosen = jnp.where(hits, jax.nn.sigmoid(logits), 0.0)
    return 2.5 * chosen / jnp.sum(chosen, axis=1, keepdims=True)


def fast_body(
    streams, phi_matrix, mix_scale, mix_bias, router, expert_index_table, w_gate, w_up, down_weight
):
    planes, exps = lax.axis_size("seq"), lax.axis_size("exp")
    pre, post, mixing = mix_coefficients(streams, phi_matrix, mix_scale, mix_bias)
    layer_in = mix_input(streams, pre)
    count, width = layer_in.shape
    local = w_gate.shape[0]
    gates = dense_gates(layer_in, router, expert_index_table)
    high = gates.astype(jnp.bfloat16)
    low = (gates - high.astype(jnp.float32)).astype(jnp.bfloat16)
    filler = jnp.zeros((count, 128 - 2 * EXPERTS), jnp.bfloat16)
    block = jnp.concatenate([layer_in, high, low, filler], axis=1)
    everyone = gather_tokens(block, planes, exps)
    owner = lax.axis_index("exp")
    tail = everyone[:, :, width:].astype(jnp.float32)
    tail = tail[:, :, :EXPERTS] + tail[:, :, EXPERTS : 2 * EXPERTS]
    mine = lax.dynamic_slice_in_dim(tail, owner * local, local, axis=2)
    mine = mine.transpose(0, 2, 1)
    taken = mine > 0
    before = (lax.iota(jnp.int32, count)[:, None] < lax.iota(jnp.int32, count)[None, :]).astype(jnp.bfloat16)
    ranks = jnp.dot(taken.astype(jnp.bfloat16).reshape(-1, count), before, preferred_element_type=jnp.float32)
    ranks = ranks.reshape(taken.shape).astype(jnp.int32)
    each = 4
    groups = planes * exps // each
    offset = (lax.iota(jnp.int32, planes * exps) % each * CAP)[:, None, None]
    spots = jnp.where(taken, ranks + offset, -1)
    spots = spots.reshape(groups, each, local, count).transpose(0, 2, 1, 3).reshape(groups, local, each * count)
    weights = mine.reshape(groups, each, local, count).transpose(0, 2, 1, 3).reshape(groups, local, each * count)
    hit = spots[:, :, None, :] == lax.iota(jnp.int32, each * CAP)[None, None, :, None]
    spread = hit.astype(jnp.bfloat16).reshape(groups, local * each * CAP, each * count)
    slot_gates = jnp.sum(jnp.where(hit, weights[:, :, None, :], 0.0), axis=3)
    slot_gates = slot_gates.transpose(1, 0, 2).reshape(local, groups * each * CAP, 1)
    parts = run_experts(
        everyone.reshape(groups, each * count, -1), spread, slot_gates, w_gate, w_up, down_weight
    )
    moe_out = scatter_sum(parts.reshape(planes * exps, count, width), planes, exps)
    return mix_output(streams, mixing, post, moe_out)


def solution(mesh):
    in_specs = (
        P(("seq", "exp"), None, None),
        P(),
        P(),
        P(),
        P(),
        P(("seq", "exp"), None),
        P("exp", None, "seq"),
        P("exp", None, "seq"),
        P("exp", "seq", None),
    )
    out_specs = P(("seq", "exp"), None, None)
    chosen = fast_body if mesh.shape["exp"] == 8 else body
    return jax.shard_map(chosen, mesh=mesh, in_specs=in_specs, out_specs=out_specs, check_vma=False)
```

```python
import functools

import jax
import jax.numpy as jnp
from jax import lax
from jax.experimental import pallas as pl
from jax.experimental.pallas import tpu as pltpu
from jax.sharding import PartitionSpec as P

BALANCE_SWEEPS = 20
EXPERTS = 32
CAP = 20
MESH = pl.DeviceIdType.MESH


def mix_coefficients(streams, phi_matrix, mix_scale, mix_bias):
    count = streams.shape[1]
    flat = streams.astype(jnp.float32).reshape(streams.shape[0], -1)
    normed = flat * lax.rsqrt(jnp.mean(flat * flat, axis=1, keepdims=True) + 1e-06)
    normed = normed.astype(jnp.bfloat16)
    coeffs = lax.dot_general(
        normed, phi_matrix, (((1,), (1,)), ((), ())), preferred_element_type=jnp.float32
    )
    pre = jax.nn.sigmoid(mix_scale[0] * coeffs[:, :count] + mix_bias[:count])
    post = 2.0 * jax.nn.sigmoid(
        mix_scale[1] * coeffs[:, count : 2 * count] + mix_bias[count : 2 * count]
    )
    logits = mix_scale[2] * coeffs[:, 2 * count :] + mix_bias[2 * count :]
    mixing = jnp.exp(logits).reshape(-1, count, count)
    for sweep_step in range(BALANCE_SWEEPS):
        mixing = mixing / jnp.sum(mixing, axis=2, keepdims=True)
        mixing = mixing / jnp.sum(mixing, axis=1, keepdims=True)
    return (pre, post, mixing)


def mix_input(streams, pre):
    total = pre[:, 0, None] * streams[:, 0, :].astype(jnp.float32)
    for stream in range(1, streams.shape[1]):
        total = total + pre[:, stream, None] * streams[:, stream, :].astype(jnp.float32)
    return total.astype(jnp.bfloat16)


def mix_output(streams, mixing, post, moe_out):
    rows = []
    for target in range(streams.shape[1]):
        total = mixing[:, target, 0, None] * streams[:, 0, :].astype(jnp.float32)
        for source in range(1, streams.shape[1]):
            total = total + mixing[:, target, source, None] * streams[:, source, :].astype(
                jnp.float32
            )
        rows.append(total + post[:, target, None] * moe_out)
    return jnp.stack(rows, axis=1).astype(jnp.bfloat16)


def route_gates(layer_in, router, expert_index_table):
    logits = lax.dot_general(
        layer_in, router, (((1,), (1,)), ((), ())), preferred_element_type=jnp.float32
    )
    affinity = jax.nn.sigmoid(logits)
    chosen = jnp.take_along_axis(affinity, expert_index_table, axis=1)
    return 2.5 * chosen / jnp.sum(chosen, axis=1, keepdims=True)


def slot_ranks(expert_index_table):
    flat = expert_index_table.reshape(-1)
    onehot = (flat[:, None] == lax.iota(jnp.int32, EXPERTS)[None, :]).astype(jnp.int32)
    prior_value = jnp.cumsum(onehot, axis=0) - onehot
    return jnp.sum(prior_value * onehot, axis=1).reshape(expert_index_table.shape)


def expert_block(blocks, w_gate, w_up, down_weight):
    count, local, slots, width = blocks.shape
    rows = blocks.transpose(1, 0, 2, 3).reshape(local, count * slots, width)
    gate_part = jnp.einsum("erd,edf->erf", rows, w_gate, preferred_element_type=jnp.float32)
    up_part = jnp.einsum("erd,edf->erf", rows, w_up, preferred_element_type=jnp.float32)
    hidden = (jax.nn.silu(gate_part) * up_part).astype(jnp.bfloat16)
    part = jnp.einsum(
        "erf,efd->erd", hidden, down_weight, preferred_element_type=jnp.float32
    ).astype(jnp.bfloat16)
    return part.reshape(local, count, slots, width).transpose(1, 0, 2, 3)


def weigh_slots(returned_rows, targets, gates):
    selected_slot = jnp.take(returned_rows, targets.reshape(-1), axis=0).astype(jnp.float32)
    selected_slot = selected_slot.reshape(
        targets.shape[0], targets.shape[1], returned_rows.shape[1]
    )
    return jnp.sum(gates[:, :, None] * selected_slot, axis=1)


def body(
    streams, phi_matrix, mix_scale, mix_bias, router, expert_index_table, w_gate, w_up, down_weight
):
    pre, post, mixing = mix_coefficients(streams, phi_matrix, mix_scale, mix_bias)
    layer_in = mix_input(streams, pre)
    width = layer_in.shape[1]
    owners = lax.axis_size("exp")
    local = w_gate.shape[0]
    column_in, column_ids = (
        lax.all_gather(layer_in, "seq", axis=0, tiled=True),
        lax.all_gather(expert_index_table, "seq", axis=0, tiled=True),
    )
    sources = lax.axis_size("seq")
    tok_count = layer_in.shape[0]
    topk = expert_index_table.shape[1]
    gates = route_gates(column_in, router, column_ids)
    ranks = jax.vmap(slot_ranks)(column_ids.reshape(sources, tok_count, topk)).reshape(
        column_ids.shape
    )
    source_lookup = (lax.iota(jnp.int32, sources * tok_count) // tok_count)[:, None]
    targets = (column_ids * sources + source_lookup) * CAP + ranks
    places = lax.iota(jnp.int32, EXPERTS * sources * CAP)
    dispatch = jnp.any(places[:, None, None] == targets[None, :, :], axis=2).astype(jnp.bfloat16)
    send = jnp.dot(dispatch, column_in, preferred_element_type=jnp.float32).astype(jnp.bfloat16)
    send = send.reshape(owners, local, sources * CAP, width)
    part = expert_block(
        lax.all_to_all(send, "exp", split_axis=0, concat_axis=0, tiled=True),
        w_gate,
        w_up,
        down_weight,
    )
    returned = lax.all_to_all(part, "exp", split_axis=0, concat_axis=0, tiled=True)
    weighted = weigh_slots(returned.reshape(-1, width), targets, gates)
    moe_out = lax.psum_scatter(
        weighted.astype(jnp.bfloat16), "seq", scatter_dimension=0, tiled=True
    ).astype(jnp.float32)
    return mix_output(streams, mixing, post, moe_out)


def swap(exp, bit):
    side = lax.rem(exp // bit, 2)
    return exp + bit - 2 * bit * side


def greet(peers):
    barrier = pltpu.get_barrier_semaphore()
    for peer in peers:
        pl.semaphore_signal(barrier, inc=1, device_id=peer, device_id_type=MESH)
    pl.semaphore_wait(barrier, len(peers))


def place(planes, exps):
    z, e = lax.axis_index("seq"), lax.axis_index("exp")
    core, x, y = swap(e, 1), swap(e, 2), swap(e, 4)
    both = swap(x, 4)
    return z, e, core, x, y, both


def gather_kernel(planes, exps, block, pick_rank, pick_gate, want, want_across, slots, slot_gates, collect,
                  out, staged, s_z, r_z, s_1, r_1, s_2, r_2, s_c, r_c, s_own, s_out):
    z, e, core, x, y, both = place(planes, exps)
    half_rows = block.shape[0] // 2
    first, second = (x, y), (y, x)
    greet([(lax.rem(z + d, planes), e) for d in range(1, planes)] + [(z, x), (z, y), (z, core)])
    started = []

    def rows(half):
        return pl.ds(half * half_rows, half_rows)

    def push(src, plane, exp, half, send, recv, target):
        copy = pltpu.make_async_remote_copy(
            src_ref=src,
            dst_ref=out.at[plane * exps + exp, rows(half)],
            send_sem=send,
            recv_sem=recv,
            device_id=target,
            device_id_type=MESH,
        )
        copy.start()
        started.append(copy)

    def arrive(plane, exp, half, sem):
        spot = out.at[plane * exps + exp, rows(half)]
        pltpu.make_async_copy(spot, spot, sem).wait()

    def plane_at(k):
        return lax.rem(z + planes - k, planes)

    def local(k, exp, half):
        if k == 0 and exp is e:
            return block.at[rows(half)]
        return out.at[plane_at(k) * exps + exp, rows(half)]

    def across(k, exp, half, index):
        push(local(k, exp, half), plane_at(k), exp, half, s_c.at[k, half, index], r_c.at[k, half, index], (z, core))

    def spread_own(k):
        for half in (0, 1):
            if k:
                arrive(plane_at(k), e, half, r_z.at[k - 1, half])
            push(local(k, e, half), plane_at(k), e, half, s_1.at[k, half], r_1.at[k, half], (z, first[half]))
            push(local(k, e, half), plane_at(k), e, half, s_2.at[k, half, 0], r_2.at[k, half, 0], (z, second[half]))
            across(k, e, half, 0)

    def spread_first(k):
        for half in (0, 1):
            arrive(plane_at(k), first[half], half, r_1.at[k, half])
            push(local(k, first[half], half), plane_at(k), first[half], half, s_2.at[k, half, 1], r_2.at[k, half, 1], (z, second[half]))
            across(k, first[half], half, 1)

    def spread_second(k):
        for half in (0, 1):
            for index, exp in enumerate((second[half], both)):
                arrive(plane_at(k), exp, half, r_2.at[k, half, index])
                across(k, exp, half, 2 + index)

    own = pltpu.make_async_copy(block, out.at[z * exps + e], s_own)
    own.start()
    for d in range(1, planes):
        for half in (0, 1):
            push(block.at[rows(half)], z, e, half, s_z.at[d - 1, half], r_z.at[d - 1, half], (lax.rem(z + d, planes), e))
    spread_own(0)
    own.wait()
    width = staged.shape[2]
    room = slot_gates.shape[2]
    each = collect.shape[1] // block.shape[0]
    side = exps // each
    wide = 896 if width % 896 == 0 else width
    stores = []

    def dispatch(group):
        blocks = pl.ds(group * each, each)
        tail = out[blocks, :, width:].reshape(collect.shape[1], 128)

        def picked(left, right):
            return lax.dot_general(left, right, (((1,), (1,)), ((), ())), preferred_element_type=jnp.float32)

        hit = picked(pick_rank[...], tail) == want[...]
        gates = jnp.sum(jnp.where(hit, picked(pick_gate[...], tail), 0.0), axis=1, keepdims=True)
        for own_expert in range(slot_gates.shape[0]):
            slot_gates[own_expert, group] = gates[own_expert * room : (own_expert + 1) * room]
        spread = jnp.where(hit, 1.0, 0.0).astype(jnp.bfloat16)
        hit_across = picked(tail, pick_rank[...]) == want_across[...]
        collect[group] = jnp.where(hit_across, 1.0, 0.0).astype(jnp.bfloat16)

        def one(i, carry):
            columns = pl.ds(pl.multiple_of(i * wide, wide), wide)
            rows_in = out[blocks, :, columns].reshape(collect.shape[1], wide)
            staged[group, :, columns] = jnp.dot(spread, rows_in, preferred_element_type=jnp.float32).astype(staged.dtype)
            return carry

        lax.fori_loop(0, width // wide, one, 0)

    def finish(k):
        for half in (0, 1):
            here = (core, swap(first[half], 1), swap(second[half], 1), swap(both, 1))
            for index, exp in enumerate(here):
                arrive(plane_at(k), exp, half, r_c.at[k, half, index])
        for part in range(side):
            group = plane_at(k) * side + part
            dispatch(group)
            store = pltpu.make_async_copy(staged.at[group], slots.at[group], s_out.at[k, part])
            store.start()
            stores.append(store)

    for k in range(1, planes + 3):
        if k < planes:
            spread_own(k)
        if k - 1 < planes:
            spread_first(k - 1)
        if 2 <= k < planes + 2:
            spread_second(k - 2)
        if k >= 3:
            finish(k - 3)
    for copy in started:
        copy.wait_send()
    for store in stores:
        store.wait()


def gather_tokens(block, pick_rank, pick_gate, want, planes, exps, local):
    dma = pltpu.SemaphoreType.DMA
    shapes = [(planes - 1, 2), (planes, 2), (planes, 2, 2), (planes, 2, 4)]
    tokens = block.shape[0]
    width = block.shape[1] - 128
    held, reach = want.shape
    each = reach // tokens
    groups = planes * exps // each
    vmem = pl.BlockSpec(memory_space=pltpu.VMEM)
    return pl.pallas_call(
        functools.partial(gather_kernel, planes, exps),
        out_shape=[
            jax.ShapeDtypeStruct((groups, held, width), block.dtype),
            jax.ShapeDtypeStruct((local, groups, held // local, 1), jnp.float32),
            jax.ShapeDtypeStruct((groups, reach, held), jnp.bfloat16),
        ],
        in_specs=[pl.BlockSpec(memory_space=pl.ANY)] + [vmem] * 4,
        out_specs=[pl.BlockSpec(memory_space=pl.ANY), vmem, vmem],
        scratch_shapes=[
            pltpu.VMEM((planes * exps,) + block.shape, block.dtype),
            pltpu.VMEM((groups, held, width), block.dtype),
        ]
        + [dma(shape) for shape in shapes for way in range(2)]
        + [dma, dma((planes, exps // each))],
        compiler_params=pltpu.CompilerParams(
            collective_id=0, has_side_effects=True, vmem_limit_bytes=52 * 1024 * 1024
        ),
        name="gather_tokens",
    )(block, pick_rank, pick_gate, want, want.T)


def scatter_kernel(planes, exps, parts, collect, out, slots, made, in_c, in_2, in_1, in_z,
                   s_own, s_c, r_c, s_2, r_2, s_1, r_1, s_z, r_z):
    z, e, core, x, y, both = place(planes, exps)
    tokens, width = out.shape
    half_rows = tokens // 2
    step = 512 if width % 512 == 0 else width
    first, second = (x, y), (y, x)
    greet([(lax.rem(z + d, planes), e) for d in range(1, planes)] + [(z, x), (z, y), (z, core)])
    started = []

    def rows(half):
        return pl.ds(half * half_rows, half_rows)

    def push(src, dst, send, recv, target):
        copy = pltpu.make_async_remote_copy(
            src_ref=src, dst_ref=dst, send_sem=send, recv_sem=recv, device_id=target, device_id_type=MESH
        )
        copy.start()
        started.append(copy)

    def arrive(spot, sem):
        pltpu.make_async_copy(spot, spot, sem).wait()

    def add(total, term):
        def one(i, carry):
            columns = pl.ds(pl.multiple_of(i * step, step), step)
            total[:, columns] = (
                total[:, columns].astype(jnp.float32) + term[:, columns].astype(jnp.float32)
            ).astype(total.dtype)
            return carry

        lax.fori_loop(0, width // step, one, 0)

    def plane_at(k):
        return lax.rem(z + k, planes)

    def dests(half):
        return (both, second[half], first[half], e)

    order = [k for k in range(1, planes)] + [0]
    each = collect.shape[1] // tokens
    side = exps // each
    wide = 896 if width % 896 == 0 else width

    def load(k, part):
        group = plane_at(k) * side + part
        return pltpu.make_async_copy(parts.at[group], slots.at[group], s_own.at[k, part])

    def held(k, half, index):
        return made.at[plane_at(k) * exps + dests(half)[index], rows(half)]

    for k in order:
        for part in range(side):
            load(k, part).start()

    def produce(k):
        for part in range(side):
            load(k, part).wait()
            group = plane_at(k) * side + part

            def one(i, carry):
                columns = pl.ds(pl.multiple_of(i * wide, wide), wide)
                total = jnp.dot(collect[group], slots[group, :, columns], preferred_element_type=jnp.float32)
                made[pl.ds(group * each, each), :, columns] = total.astype(made.dtype).reshape(each, tokens, wide)
                return carry

            lax.fori_loop(0, width // wide, one, 0)
        for half in (0, 1):
            for index, exp in enumerate(dests(half)):
                away = made.at[plane_at(k) * exps + swap(exp, 1), rows(half)]
                push(away, in_c.at[k, half, index], s_c.at[k, half, index], r_c.at[k, half, index], (z, core))

    def merge_core(k):
        for half in (0, 1):
            for index in range(4):
                arrive(in_c.at[k, half, index], r_c.at[k, half, index])
                add(held(k, half, index), in_c.at[k, half, index])
                if index < 2:
                    push(held(k, half, index), in_2.at[k, half, index], s_2.at[k, half, index], r_2.at[k, half, index], (z, second[half]))

    def merge_second(k):
        for half in (0, 1):
            for index in (0, 1):
                arrive(in_2.at[k, half, index], r_2.at[k, half, index])
                add(held(k, half, 2 + index), in_2.at[k, half, index])
                if index == 0:
                    push(held(k, half, 2), in_1.at[k, half], s_1.at[k, half], r_1.at[k, half], (z, first[half]))

    def merge_first(k):
        for half in (0, 1):
            arrive(in_1.at[k, half], r_1.at[k, half])
            add(held(k, half, 3), in_1.at[k, half])
            if k:
                push(held(k, half, 3), in_z.at[k - 1, half], s_z.at[k - 1, half], r_z.at[k - 1, half], (plane_at(k), e))

    for turn in range(planes + 3):
        if turn < planes:
            produce(order[turn])
        if 1 <= turn <= planes:
            merge_core(order[turn - 1])
        if 2 <= turn <= planes + 1:
            merge_second(order[turn - 2])
        if turn >= 3:
            merge_first(order[turn - 3])
    for k in range(1, planes):
        for half in (0, 1):
            arrive(in_z.at[k - 1, half], r_z.at[k - 1, half])
    for half in (0, 1):
        def one(i, carry):
            columns = pl.ds(pl.multiple_of(i * step, step), step)
            total = made[z * exps + e, rows(half), columns].astype(jnp.float32)
            for k in range(1, planes):
                total = total + in_z[k - 1, half, :, columns].astype(jnp.float32)
            out[half * half_rows : (half + 1) * half_rows, columns] = total
            return carry

        lax.fori_loop(0, width // step, one, 0)
    for copy in started:
        copy.wait_send()


def scatter_sum(parts, collect, planes, exps):
    groups, held, width = parts.shape
    tokens = collect.shape[1] * groups // (planes * exps)
    dma = pltpu.SemaphoreType.DMA
    half = (tokens // 2, width)
    shapes = [(planes, 2, 4), (planes, 2, 2), (planes, 2), (planes - 1, 2)]
    vmem = pl.BlockSpec(memory_space=pltpu.VMEM)
    return pl.pallas_call(
        functools.partial(scatter_kernel, planes, exps),
        out_shape=jax.ShapeDtypeStruct((tokens, width), jnp.float32),
        in_specs=[pl.BlockSpec(memory_space=pl.ANY), vmem],
        out_specs=vmem,
        scratch_shapes=[
            pltpu.VMEM(parts.shape, parts.dtype),
            pltpu.VMEM((planes * exps, tokens, width), parts.dtype),
        ]
        + [pltpu.VMEM(shape + half, parts.dtype) for shape in shapes]
        + [dma((planes, groups // planes))]
        + [dma(shape) for shape in shapes for way in range(2)],
        compiler_params=pltpu.CompilerParams(
            collective_id=1, has_side_effects=True, vmem_limit_bytes=58 * 1024 * 1024
        ),
        name="scatter_sum",
    )(parts, collect)


def expert_kernel(slots, slot_gates, w_gate, w_up, w_down, out, hidden):
    groups, room, width = slots.shape
    ff = hidden.shape[1]
    wide = 896 if width % 896 == 0 else width
    tall = 256 if ff % 256 == 0 else ff
    gates = slot_gates[0].reshape(groups * room, 1)
    for i in range(ff // tall):
        columns = pl.ds(i * tall, tall)
        rows = slots[...].reshape(groups * room, width)
        gate_part = jnp.dot(rows, w_gate[0, :, columns], preferred_element_type=jnp.float32)
        up_part = jnp.dot(rows, w_up[0, :, columns], preferred_element_type=jnp.float32)
        hidden[:, columns] = (
            gate_part / (1.0 + jnp.exp(-gate_part)) * up_part * gates
        ).astype(hidden.dtype)

    def down(i, carry):
        columns = pl.ds(pl.multiple_of(i * wide, wide), wide)
        part = jnp.dot(hidden[...], w_down[0, :, columns], preferred_element_type=jnp.float32)
        out[:, :, columns] = part.astype(out.dtype).reshape(groups, room, wide)
        return carry

    lax.fori_loop(0, width // wide, down, 0)


def run_experts(slots, slot_gates, w_gate, w_up, down_weight):
    groups, held, width = slots.shape
    local, _, ff = w_gate.shape
    room = held // local
    rows = pl.BlockSpec((groups, room, width), lambda i: (0, i, 0))

    def each(array):
        return pl.BlockSpec((1,) + array.shape[1:], lambda i: (i,) + (0,) * (array.ndim - 1))

    return pl.pallas_call(
        expert_kernel,
        grid=(local,),
        out_shape=jax.ShapeDtypeStruct(slots.shape, jnp.bfloat16),
        in_specs=[rows] + [each(a) for a in (slot_gates, w_gate, w_up, down_weight)],
        out_specs=rows,
        scratch_shapes=[pltpu.VMEM((groups * room, ff), jnp.bfloat16)],
        compiler_params=pltpu.CompilerParams(
            dimension_semantics=("arbitrary",), vmem_limit_bytes=60 * 1024 * 1024
        ),
        name="run_experts",
    )(slots, slot_gates, w_gate, w_up, down_weight)


def dense_gates(layer_in, router, expert_index_table):
    logits = lax.dot_general(
        layer_in, router, (((1,), (1,)), ((), ())), preferred_element_type=jnp.float32
    )
    names = lax.iota(jnp.int32, EXPERTS)
    hits = jnp.any(expert_index_table[:, :, None] == names[None, None, :], axis=1)
    chosen = jnp.where(hits, jax.nn.sigmoid(logits), 0.0)
    count = hits.shape[0]
    before = (lax.iota(jnp.int32, count)[:, None] > lax.iota(jnp.int32, count)[None, :]).astype(jnp.bfloat16)
    ranks = jnp.dot(before, hits.astype(jnp.bfloat16), preferred_element_type=jnp.float32) + 1.0
    gates = 2.5 * chosen / jnp.sum(chosen, axis=1, keepdims=True)
    return gates, jnp.where(hits, ranks, 0.0).astype(jnp.bfloat16)


def fast_body(
    streams, phi_matrix, mix_scale, mix_bias, router, expert_index_table, w_gate, w_up, down_weight
):
    planes, exps = lax.axis_size("seq"), lax.axis_size("exp")
    pre, post, mixing = mix_coefficients(streams, phi_matrix, mix_scale, mix_bias)
    layer_in = mix_input(streams, pre)
    count, width = layer_in.shape
    local = w_gate.shape[0]
    gates, ranks = dense_gates(layer_in, router, expert_index_table)
    high = gates.astype(jnp.bfloat16)
    low = (gates - high.astype(jnp.float32)).astype(jnp.bfloat16)
    filler = jnp.zeros((count, 128 - 3 * EXPERTS), jnp.bfloat16)
    block = jnp.concatenate([layer_in, high, low, ranks, filler], axis=1)
    each = 4
    room = each * CAP
    named = lax.axis_index("exp") * local + lax.iota(jnp.int32, local * room) // room
    column = lax.iota(jnp.int32, 128)[None, :]
    pick_gate = ((column == named[:, None]) | (column == named[:, None] + EXPERTS)).astype(jnp.bfloat16)
    pick_rank = (column == named[:, None] + 2 * EXPERTS).astype(jnp.bfloat16)
    spot = lax.iota(jnp.int32, local * room) % room
    source = lax.iota(jnp.int32, each * count) // count
    want = jnp.where(spot[:, None] // CAP == source[None, :], spot[:, None] % CAP + 1, -1).astype(jnp.float32)
    slots, slot_gates, collect = gather_tokens(block, pick_rank, pick_gate, want, planes, exps, local)
    parts = run_experts(slots, slot_gates, w_gate, w_up, down_weight)
    moe_out = scatter_sum(parts, collect, planes, exps)
    return mix_output(streams, mixing, post, moe_out)


def solution(mesh):
    in_specs = (
        P(("seq", "exp"), None, None),
        P(),
        P(),
        P(),
        P(),
        P(("seq", "exp"), None),
        P("exp", None, "seq"),
        P("exp", None, "seq"),
        P("exp", "seq", None),
    )
    out_specs = P(("seq", "exp"), None, None)
    chosen = fast_body if mesh.shape["exp"] == 8 else body
    return jax.shard_map(chosen, mesh=mesh, in_specs=in_specs, out_specs=out_specs, check_vma=False)
```

```python
import functools

import jax
import jax.numpy as jnp
from jax import lax
from jax.experimental import pallas as pl
from jax.experimental.pallas import tpu as pltpu
from jax.sharding import PartitionSpec as P

BALANCE_SWEEPS = 20
EXPERTS = 32
CAP = 20
MESH = pl.DeviceIdType.MESH


def mix_coefficients(streams, phi_matrix, mix_scale, mix_bias):
    count = streams.shape[1]
    flat = streams.astype(jnp.float32).reshape(streams.shape[0], -1)
    normed = flat * lax.rsqrt(jnp.mean(flat * flat, axis=1, keepdims=True) + 1e-06)
    normed = normed.astype(jnp.bfloat16)
    coeffs = lax.dot_general(
        normed, phi_matrix, (((1,), (1,)), ((), ())), preferred_element_type=jnp.float32
    )
    pre = jax.nn.sigmoid(mix_scale[0] * coeffs[:, :count] + mix_bias[:count])
    post = 2.0 * jax.nn.sigmoid(
        mix_scale[1] * coeffs[:, count : 2 * count] + mix_bias[count : 2 * count]
    )
    logits = mix_scale[2] * coeffs[:, 2 * count :] + mix_bias[2 * count :]
    mixing = jnp.exp(logits).reshape(-1, count, count)
    for sweep_step in range(BALANCE_SWEEPS):
        mixing = mixing / jnp.sum(mixing, axis=2, keepdims=True)
        mixing = mixing / jnp.sum(mixing, axis=1, keepdims=True)
    return (pre, post, mixing)


def mix_input(streams, pre):
    total = pre[:, 0, None] * streams[:, 0, :].astype(jnp.float32)
    for stream in range(1, streams.shape[1]):
        total = total + pre[:, stream, None] * streams[:, stream, :].astype(jnp.float32)
    return total.astype(jnp.bfloat16)


def mix_output(streams, mixing, post, moe_out):
    rows = []
    for target in range(streams.shape[1]):
        total = mixing[:, target, 0, None] * streams[:, 0, :].astype(jnp.float32)
        for source in range(1, streams.shape[1]):
            total = total + mixing[:, target, source, None] * streams[:, source, :].astype(
                jnp.float32
            )
        rows.append(total + post[:, target, None] * moe_out)
    return jnp.stack(rows, axis=1).astype(jnp.bfloat16)


def route_gates(layer_in, router, expert_index_table):
    logits = lax.dot_general(
        layer_in, router, (((1,), (1,)), ((), ())), preferred_element_type=jnp.float32
    )
    affinity = jax.nn.sigmoid(logits)
    chosen = jnp.take_along_axis(affinity, expert_index_table, axis=1)
    return 2.5 * chosen / jnp.sum(chosen, axis=1, keepdims=True)


def slot_ranks(expert_index_table):
    flat = expert_index_table.reshape(-1)
    onehot = (flat[:, None] == lax.iota(jnp.int32, EXPERTS)[None, :]).astype(jnp.int32)
    prior_value = jnp.cumsum(onehot, axis=0) - onehot
    return jnp.sum(prior_value * onehot, axis=1).reshape(expert_index_table.shape)


def expert_block(blocks, w_gate, w_up, down_weight):
    count, local, slots, width = blocks.shape
    rows = blocks.transpose(1, 0, 2, 3).reshape(local, count * slots, width)
    gate_part = jnp.einsum("erd,edf->erf", rows, w_gate, preferred_element_type=jnp.float32)
    up_part = jnp.einsum("erd,edf->erf", rows, w_up, preferred_element_type=jnp.float32)
    hidden = (jax.nn.silu(gate_part) * up_part).astype(jnp.bfloat16)
    part = jnp.einsum(
        "erf,efd->erd", hidden, down_weight, preferred_element_type=jnp.float32
    ).astype(jnp.bfloat16)
    return part.reshape(local, count, slots, width).transpose(1, 0, 2, 3)


def weigh_slots(returned_rows, targets, gates):
    selected_slot = jnp.take(returned_rows, targets.reshape(-1), axis=0).astype(jnp.float32)
    selected_slot = selected_slot.reshape(
        targets.shape[0], targets.shape[1], returned_rows.shape[1]
    )
    return jnp.sum(gates[:, :, None] * selected_slot, axis=1)


def body(
    streams, phi_matrix, mix_scale, mix_bias, router, expert_index_table, w_gate, w_up, down_weight
):
    pre, post, mixing = mix_coefficients(streams, phi_matrix, mix_scale, mix_bias)
    layer_in = mix_input(streams, pre)
    width = layer_in.shape[1]
    owners = lax.axis_size("exp")
    local = w_gate.shape[0]
    column_in, column_ids = (
        lax.all_gather(layer_in, "seq", axis=0, tiled=True),
        lax.all_gather(expert_index_table, "seq", axis=0, tiled=True),
    )
    sources = lax.axis_size("seq")
    tok_count = layer_in.shape[0]
    topk = expert_index_table.shape[1]
    gates = route_gates(column_in, router, column_ids)
    ranks = jax.vmap(slot_ranks)(column_ids.reshape(sources, tok_count, topk)).reshape(
        column_ids.shape
    )
    source_lookup = (lax.iota(jnp.int32, sources * tok_count) // tok_count)[:, None]
    targets = (column_ids * sources + source_lookup) * CAP + ranks
    places = lax.iota(jnp.int32, EXPERTS * sources * CAP)
    dispatch = jnp.any(places[:, None, None] == targets[None, :, :], axis=2).astype(jnp.bfloat16)
    send = jnp.dot(dispatch, column_in, preferred_element_type=jnp.float32).astype(jnp.bfloat16)
    send = send.reshape(owners, local, sources * CAP, width)
    part = expert_block(
        lax.all_to_all(send, "exp", split_axis=0, concat_axis=0, tiled=True),
        w_gate,
        w_up,
        down_weight,
    )
    returned = lax.all_to_all(part, "exp", split_axis=0, concat_axis=0, tiled=True)
    weighted = weigh_slots(returned.reshape(-1, width), targets, gates)
    moe_out = lax.psum_scatter(
        weighted.astype(jnp.bfloat16), "seq", scatter_dimension=0, tiled=True
    ).astype(jnp.float32)
    return mix_output(streams, mixing, post, moe_out)


def swap(exp, bit):
    side = lax.rem(exp // bit, 2)
    return exp + bit - 2 * bit * side


def partner(plane, k):
    bit = 1
    while bit <= k:
        if k & bit:
            plane = swap(plane, bit)
        bit *= 2
    return plane


def greet(peers):
    barrier = pltpu.get_barrier_semaphore()
    for peer in peers:
        pl.semaphore_signal(barrier, inc=1, device_id=peer, device_id_type=MESH)
    pl.semaphore_wait(barrier, len(peers))


def place(planes, exps):
    z, e = lax.axis_index("seq"), lax.axis_index("exp")
    core, x, y = swap(e, 1), swap(e, 2), swap(e, 4)
    both = swap(x, 4)
    return z, e, core, x, y, both


def gather_kernel(planes, exps, block, pick_rank, pick_gate, want, want_across, slots, slot_gates, collect,
                  out, staged, s_z, r_z, s_1, r_1, s_2, r_2, s_c, r_c, s_own, s_out):
    z, e, core, x, y, both = place(planes, exps)
    half_rows = block.shape[0] // 2
    first, second = (x, y), (y, x)
    greet([(partner(z, d), e) for d in range(1, planes)] + [(z, x), (z, y), (z, core)])
    started = []

    def rows(half):
        return pl.ds(half * half_rows, half_rows)

    def push(src, plane, exp, half, send, recv, target):
        copy = pltpu.make_async_remote_copy(
            src_ref=src,
            dst_ref=out.at[plane * exps + exp, rows(half)],
            send_sem=send,
            recv_sem=recv,
            device_id=target,
            device_id_type=MESH,
        )
        copy.start()
        started.append(copy)

    def arrive(plane, exp, half, sem):
        spot = out.at[plane * exps + exp, rows(half)]
        pltpu.make_async_copy(spot, spot, sem).wait()

    def plane_at(k):
        return partner(z, k)

    def local(k, exp, half):
        if k == 0 and exp is e:
            return block.at[rows(half)]
        return out.at[plane_at(k) * exps + exp, rows(half)]

    def across(k, exp, half, index):
        push(local(k, exp, half), plane_at(k), exp, half, s_c.at[k, half, index], r_c.at[k, half, index], (z, core))

    def spread_own(k):
        for half in (0, 1):
            if k:
                arrive(plane_at(k), e, half, r_z.at[k - 1, half])
            push(local(k, e, half), plane_at(k), e, half, s_1.at[k, half], r_1.at[k, half], (z, first[half]))
            push(local(k, e, half), plane_at(k), e, half, s_2.at[k, half, 0], r_2.at[k, half, 0], (z, second[half]))
            across(k, e, half, 0)

    def spread_first(k):
        for half in (0, 1):
            arrive(plane_at(k), first[half], half, r_1.at[k, half])
            push(local(k, first[half], half), plane_at(k), first[half], half, s_2.at[k, half, 1], r_2.at[k, half, 1], (z, second[half]))
            across(k, first[half], half, 1)

    def spread_second(k):
        for half in (0, 1):
            for index, exp in enumerate((second[half], both)):
                arrive(plane_at(k), exp, half, r_2.at[k, half, index])
                across(k, exp, half, 2 + index)

    own = pltpu.make_async_copy(block, out.at[z * exps + e], s_own)
    own.start()
    for d in range(1, planes):
        for half in (0, 1):
            push(block.at[rows(half)], z, e, half, s_z.at[d - 1, half], r_z.at[d - 1, half], (partner(z, d), e))
    spread_own(0)
    own.wait()
    width = staged.shape[2]
    room = slot_gates.shape[2]
    each = collect.shape[1] // block.shape[0]
    side = exps // each
    wide = 896 if width % 896 == 0 else width
    stores = []

    def dispatch(group):
        blocks = pl.ds(group * each, each)
        tail = out[blocks, :, width:].reshape(collect.shape[1], 128)

        def picked(left, right):
            return lax.dot_general(left, right, (((1,), (1,)), ((), ())), preferred_element_type=jnp.float32)

        hit = picked(pick_rank[...], tail) == want[...]
        gates = jnp.sum(jnp.where(hit, picked(pick_gate[...], tail), 0.0), axis=1, keepdims=True)
        for own_expert in range(slot_gates.shape[0]):
            slot_gates[own_expert, group] = gates[own_expert * room : (own_expert + 1) * room]
        spread = jnp.where(hit, 1.0, 0.0).astype(jnp.bfloat16)
        hit_across = picked(tail, pick_rank[...]) == want_across[...]
        collect[group] = jnp.where(hit_across, 1.0, 0.0).astype(jnp.bfloat16)

        def one(i, carry):
            columns = pl.ds(pl.multiple_of(i * wide, wide), wide)
            rows_in = out[blocks, :, columns].reshape(collect.shape[1], wide)
            staged[group, :, columns] = jnp.dot(spread, rows_in, preferred_element_type=jnp.float32).astype(staged.dtype)
            return carry

        lax.fori_loop(0, width // wide, one, 0)

    def finish(k):
        for half in (0, 1):
            here = (core, swap(first[half], 1), swap(second[half], 1), swap(both, 1))
            for index, exp in enumerate(here):
                arrive(plane_at(k), exp, half, r_c.at[k, half, index])
        for part in range(side):
            group = plane_at(k) * side + part
            dispatch(group)
            store = pltpu.make_async_copy(staged.at[group], slots.at[group], s_out.at[k, part])
            store.start()
            stores.append(store)

    for k in range(1, planes + 3):
        if k - 1 < planes:
            spread_first(k - 1)
        if k < planes:
            spread_own(k)
        if 2 <= k < planes + 2:
            spread_second(k - 2)
        if k >= 3:
            finish(k - 3)
    for copy in started:
        copy.wait_send()
    for store in stores:
        store.wait()


def gather_tokens(block, pick_rank, pick_gate, want, planes, exps, local):
    dma = pltpu.SemaphoreType.DMA
    shapes = [(planes - 1, 2), (planes, 2), (planes, 2, 2), (planes, 2, 4)]
    tokens = block.shape[0]
    width = block.shape[1] - 128
    held, reach = want.shape
    each = reach // tokens
    groups = planes * exps // each
    vmem = pl.BlockSpec(memory_space=pltpu.VMEM)
    return pl.pallas_call(
        functools.partial(gather_kernel, planes, exps),
        out_shape=[
            jax.ShapeDtypeStruct((groups, held, width), block.dtype),
            jax.ShapeDtypeStruct((local, groups, held // local, 1), jnp.float32),
            jax.ShapeDtypeStruct((groups, reach, held), jnp.bfloat16),
        ],
        in_specs=[pl.BlockSpec(memory_space=pl.ANY)] + [vmem] * 4,
        out_specs=[pl.BlockSpec(memory_space=pl.ANY), vmem, vmem],
        scratch_shapes=[
            pltpu.VMEM((planes * exps,) + block.shape, block.dtype),
            pltpu.VMEM((groups, held, width), block.dtype),
        ]
        + [dma(shape) for shape in shapes for way in range(2)]
        + [dma, dma((planes, exps // each))],
        compiler_params=pltpu.CompilerParams(
            collective_id=0, has_side_effects=True, vmem_limit_bytes=52 * 1024 * 1024
        ),
        name="gather_tokens",
    )(block, pick_rank, pick_gate, want, want.T)


def scatter_kernel(planes, exps, parts, collect, out, slots, made, in_c, in_2, in_1, in_z,
                   s_own, s_c, r_c, s_2, r_2, s_1, r_1, s_z, r_z):
    z, e, core, x, y, both = place(planes, exps)
    tokens, width = out.shape
    half_rows = tokens // 2
    step = 512 if width % 512 == 0 else width
    first, second = (x, y), (y, x)
    greet([(partner(z, d), e) for d in range(1, planes)] + [(z, x), (z, y), (z, core)])
    started = []

    def rows(half):
        return pl.ds(half * half_rows, half_rows)

    def push(src, dst, send, recv, target):
        copy = pltpu.make_async_remote_copy(
            src_ref=src, dst_ref=dst, send_sem=send, recv_sem=recv, device_id=target, device_id_type=MESH
        )
        copy.start()
        started.append(copy)

    def arrive(spot, sem):
        pltpu.make_async_copy(spot, spot, sem).wait()

    def add(total, term):
        def one(i, carry):
            columns = pl.ds(pl.multiple_of(i * step, step), step)
            total[:, columns] = (
                total[:, columns].astype(jnp.float32) + term[:, columns].astype(jnp.float32)
            ).astype(total.dtype)
            return carry

        lax.fori_loop(0, width // step, one, 0)

    def plane_at(k):
        return partner(z, k)

    def dests(half):
        return (both, second[half], first[half], e)

    order = [k for k in range(planes - 1, -1, -1)]
    each = collect.shape[1] // tokens
    side = exps // each
    wide = 896 if width % 896 == 0 else width

    def load(k, part):
        group = plane_at(k) * side + part
        return pltpu.make_async_copy(parts.at[group], slots.at[group], s_own.at[k, part])

    def held(k, half, index):
        return made.at[plane_at(k) * exps + dests(half)[index], rows(half)]

    for k in order:
        for part in range(side):
            load(k, part).start()

    def produce(k):
        for part in range(side):
            load(k, part).wait()
            group = plane_at(k) * side + part

            def one(i, carry):
                columns = pl.ds(pl.multiple_of(i * wide, wide), wide)
                total = jnp.dot(collect[group], slots[group, :, columns], preferred_element_type=jnp.float32)
                made[pl.ds(group * each, each), :, columns] = total.astype(made.dtype).reshape(each, tokens, wide)
                return carry

            lax.fori_loop(0, width // wide, one, 0)
        for half in (0, 1):
            for index, exp in enumerate(dests(half)):
                away = made.at[plane_at(k) * exps + swap(exp, 1), rows(half)]
                push(away, in_c.at[k, half, index], s_c.at[k, half, index], r_c.at[k, half, index], (z, core))

    def merge_core(k):
        for half in (0, 1):
            for index in range(4):
                arrive(in_c.at[k, half, index], r_c.at[k, half, index])
                add(held(k, half, index), in_c.at[k, half, index])
                if index < 2:
                    push(held(k, half, index), in_2.at[k, half, index], s_2.at[k, half, index], r_2.at[k, half, index], (z, second[half]))

    def merge_second(k):
        for half in (0, 1):
            for index in (0, 1):
                arrive(in_2.at[k, half, index], r_2.at[k, half, index])
                add(held(k, half, 2 + index), in_2.at[k, half, index])
                if index == 0:
                    push(held(k, half, 2), in_1.at[k, half], s_1.at[k, half], r_1.at[k, half], (z, first[half]))

    def merge_first(k):
        for half in (0, 1):
            arrive(in_1.at[k, half], r_1.at[k, half])
            add(held(k, half, 3), in_1.at[k, half])
            if k:
                push(held(k, half, 3), in_z.at[k - 1, half], s_z.at[k - 1, half], r_z.at[k - 1, half], (plane_at(k), e))

    for turn in range(planes + 3):
        if turn < planes:
            produce(order[turn])
        if 1 <= turn <= planes:
            merge_core(order[turn - 1])
        if turn >= 3:
            merge_first(order[turn - 3])
        if 2 <= turn <= planes + 1:
            merge_second(order[turn - 2])
    for k in range(1, planes):
        for half in (0, 1):
            arrive(in_z.at[k - 1, half], r_z.at[k - 1, half])
    for half in (0, 1):
        def one(i, carry):
            columns = pl.ds(pl.multiple_of(i * step, step), step)
            total = made[z * exps + e, rows(half), columns].astype(jnp.float32)
            for k in range(1, planes):
                total = total + in_z[k - 1, half, :, columns].astype(jnp.float32)
            out[half * half_rows : (half + 1) * half_rows, columns] = total
            return carry

        lax.fori_loop(0, width // step, one, 0)
    for copy in started:
        copy.wait_send()


def scatter_sum(parts, collect, planes, exps):
    groups, held, width = parts.shape
    tokens = collect.shape[1] * groups // (planes * exps)
    dma = pltpu.SemaphoreType.DMA
    half = (tokens // 2, width)
    shapes = [(planes, 2, 4), (planes, 2, 2), (planes, 2), (planes - 1, 2)]
    vmem = pl.BlockSpec(memory_space=pltpu.VMEM)
    return pl.pallas_call(
        functools.partial(scatter_kernel, planes, exps),
        out_shape=jax.ShapeDtypeStruct((tokens, width), jnp.float32),
        in_specs=[pl.BlockSpec(memory_space=pl.ANY), vmem],
        out_specs=vmem,
        scratch_shapes=[
            pltpu.VMEM(parts.shape, parts.dtype),
            pltpu.VMEM((planes * exps, tokens, width), parts.dtype),
        ]
        + [pltpu.VMEM(shape + half, parts.dtype) for shape in shapes]
        + [dma((planes, groups // planes))]
        + [dma(shape) for shape in shapes for way in range(2)],
        compiler_params=pltpu.CompilerParams(
            collective_id=1, has_side_effects=True, vmem_limit_bytes=58 * 1024 * 1024
        ),
        name="scatter_sum",
    )(parts, collect)


def expert_kernel(slots, slot_gates, w_gate, w_up, w_down, out, hidden):
    groups, room, width = slots.shape
    ff = hidden.shape[1]
    wide = 896 if width % 896 == 0 else width
    tall = 256 if ff % 256 == 0 else ff
    gates = slot_gates[0].reshape(groups * room, 1)
    for i in range(ff // tall):
        columns = pl.ds(i * tall, tall)
        rows = slots[...].reshape(groups * room, width)
        gate_part = jnp.dot(rows, w_gate[0, :, columns], preferred_element_type=jnp.float32)
        up_part = jnp.dot(rows, w_up[0, :, columns], preferred_element_type=jnp.float32)
        hidden[:, columns] = (
            gate_part / (1.0 + jnp.exp(-gate_part)) * up_part * gates
        ).astype(hidden.dtype)

    def down(i, carry):
        columns = pl.ds(pl.multiple_of(i * wide, wide), wide)
        part = jnp.dot(hidden[...], w_down[0, :, columns], preferred_element_type=jnp.float32)
        out[:, :, columns] = part.astype(out.dtype).reshape(groups, room, wide)
        return carry

    lax.fori_loop(0, width // wide, down, 0)


def run_experts(slots, slot_gates, w_gate, w_up, down_weight):
    groups, held, width = slots.shape
    local, _, ff = w_gate.shape
    room = held // local
    rows = pl.BlockSpec((groups, room, width), lambda i: (0, i, 0))

    def each(array):
        return pl.BlockSpec((1,) + array.shape[1:], lambda i: (i,) + (0,) * (array.ndim - 1))

    return pl.pallas_call(
        expert_kernel,
        grid=(local,),
        out_shape=jax.ShapeDtypeStruct(slots.shape, jnp.bfloat16),
        in_specs=[rows] + [each(a) for a in (slot_gates, w_gate, w_up, down_weight)],
        out_specs=rows,
        scratch_shapes=[pltpu.VMEM((groups * room, ff), jnp.bfloat16)],
        compiler_params=pltpu.CompilerParams(
            dimension_semantics=("arbitrary",), vmem_limit_bytes=60 * 1024 * 1024
        ),
        name="run_experts",
    )(slots, slot_gates, w_gate, w_up, down_weight)


def dense_gates(layer_in, router, expert_index_table):
    logits = lax.dot_general(
        layer_in, router, (((1,), (1,)), ((), ())), preferred_element_type=jnp.float32
    )
    names = lax.iota(jnp.int32, EXPERTS)
    hits = jnp.any(expert_index_table[:, :, None] == names[None, None, :], axis=1)
    chosen = jnp.where(hits, jax.nn.sigmoid(logits), 0.0)
    count = hits.shape[0]
    before = (lax.iota(jnp.int32, count)[:, None] > lax.iota(jnp.int32, count)[None, :]).astype(jnp.bfloat16)
    ranks = jnp.dot(before, hits.astype(jnp.bfloat16), preferred_element_type=jnp.float32) + 1.0
    gates = 2.5 * chosen / jnp.sum(chosen, axis=1, keepdims=True)
    return gates, jnp.where(hits, ranks, 0.0).astype(jnp.bfloat16)


def fast_body(
    streams, phi_matrix, mix_scale, mix_bias, router, expert_index_table, w_gate, w_up, down_weight
):
    planes, exps = lax.axis_size("seq"), lax.axis_size("exp")
    pre, post, mixing = mix_coefficients(streams, phi_matrix, mix_scale, mix_bias)
    layer_in = mix_input(streams, pre)
    count, width = layer_in.shape
    local = w_gate.shape[0]
    gates, ranks = dense_gates(layer_in, router, expert_index_table)
    high = gates.astype(jnp.bfloat16)
    low = (gates - high.astype(jnp.float32)).astype(jnp.bfloat16)
    filler = jnp.zeros((count, 128 - 3 * EXPERTS), jnp.bfloat16)
    block = jnp.concatenate([layer_in, high, low, ranks, filler], axis=1)
    each = 4
    room = each * CAP
    named = lax.axis_index("exp") * local + lax.iota(jnp.int32, local * room) // room
    column = lax.iota(jnp.int32, 128)[None, :]
    pick_gate = ((column == named[:, None]) | (column == named[:, None] + EXPERTS)).astype(jnp.bfloat16)
    pick_rank = (column == named[:, None] + 2 * EXPERTS).astype(jnp.bfloat16)
    spot = lax.iota(jnp.int32, local * room) % room
    source = lax.iota(jnp.int32, each * count) // count
    want = jnp.where(spot[:, None] // CAP == source[None, :], spot[:, None] % CAP + 1, -1).astype(jnp.float32)
    slots, slot_gates, collect = gather_tokens(block, pick_rank, pick_gate, want, planes, exps, local)
    parts = run_experts(slots, slot_gates, w_gate, w_up, down_weight)
    moe_out = scatter_sum(parts, collect, planes, exps)
    return mix_output(streams, mixing, post, moe_out)


def solution(mesh):
    in_specs = (
        P(("seq", "exp"), None, None),
        P(),
        P(),
        P(),
        P(),
        P(("seq", "exp"), None),
        P("exp", None, "seq"),
        P("exp", None, "seq"),
        P("exp", "seq", None),
    )
    out_specs = P(("seq", "exp"), None, None)
    chosen = fast_body if (mesh.shape["seq"], mesh.shape["exp"]) == (4, 8) else body
    return jax.shard_map(chosen, mesh=mesh, in_specs=in_specs, out_specs=out_specs, check_vma=False)
```
